32 devices in a mesh: blk: 8 (over z, core), rep: 4 (over y, x).
Axes of the slice: x: 2, y: 2, z: 4, core: 2. Of those that a mesh axis runs over, the one named last changes fastest.
Arguments:
- features: bfloat16 [24576, 256], P(('blk', 'rep')), may hold values from -6 to 6
- grad_out: bfloat16 [24576, 256], P(('blk', 'rep')), may hold values from -6 to 6
- weight: bfloat16 [256, 256], replicated, may hold values from -0.375 to 0.375
- edge_tiles: bfloat16 [8, 4, 24, 2, 128, 128], P('blk', 'rep'), may hold values from 0 to 0.083984375
- tile_cols: int32 [8, 4, 24, 2], P('blk', 'rep'), may hold values from 0 to 47
- tile_live: int32 [8, 4, 24, 2], P('blk', 'rep'), may hold values 0 or 1
Outputs:
- activations: bfloat16 [24576, 256], P(('blk', 'rep'))
- grad_features: bfloat16 [24576, 256], P(('blk', 'rep'))
- grad_weight: float32 [256, 256], replicated
The draws below stay inside these ranges and needn't reach their ends.
All inputs are finite; a program needn't handle non-finite values. No bound on the sum of `tile_live` on one device may be relied on, other than what follows from the above.
Results may differ from the reference program's by a relative error of at most 0.014.
Values may be sent and summed in bfloat16 or wider, within the bound.
A program may use at most 128 MiB of HBM per device.

```python
import math
import jax
import jax.numpy as jnp
from jax import lax

D = 256
TILE = 128
ROWS_DEV = 768
TPR = 2
NODES = 24576
PANEL_BLOCKS = 24
SLICE_BLOCKS = 48
N_BLK = 8
N_REP = 4


def touch_ends(array, stream_key, low, high):
    longest = array.shape.index(max(array.shape))
    spots = []
    for shift in (0, 1):
        where = [jax.random.randint(jax.random.fold_in(stream_key, axis), (), 0, length) for axis, length in enumerate(array.shape)]
        where[longest] = (where[longest] + shift) % array.shape[longest]
        spots.append(tuple(where))
    return array.at[spots[0]].set(low).at[spots[1]].set(high)


def levels(key, dims, cuts, smallest, largest):
    level = 1.0
    for position, shards_of in cuts:
        draws = jax.random.uniform(jax.random.fold_in(jax.random.fold_in(key, 6), position), (shards_of,), jnp.float32, smallest / len(cuts), largest / len(cuts))
        level = level * jnp.repeat(jnp.exp(draws), dims[position] // shards_of).reshape((-1,) + (1,) * (len(dims) - 1 - position))
    return level


def noise(key, dims, spread, bound, split=(), kind=jnp.bfloat16):
    array = spread * jax.random.normal(key, dims, jnp.float32)
    if split:
        array = array * levels(key, dims, split, -0.22, 0.18)
    return jnp.clip(array, -bound, bound).astype(kind)


def setup_inputs(seed: int = 0) -> dict:
    key_of = jax.random.split(jax.random.key(seed), 7)
    features = noise(key_of[0], (NODES, D), 1.0, 6.0, ((0, 32),))
    grad_out = noise(key_of[1], (NODES, D), 1.0, 6.0, ((0, 32),))
    weight = noise(key_of[2], (D, D), D ** -0.5, 0.375)
    edge_tiles = jnp.clip(0.083984375 * jax.random.uniform(key_of[3], (N_BLK, N_REP, PANEL_BLOCKS, TPR, TILE, TILE), jnp.float32) ** levels(key_of[3], (N_BLK, N_REP, PANEL_BLOCKS, TPR, TILE, TILE), ((0, 8), (1, 4)), -0.2, 0.2), 0.0, 0.083984375).astype(jnp.bfloat16)
    tile_cols = touch_ends(jax.random.randint(key_of[4], (N_BLK, N_REP, PANEL_BLOCKS, TPR), 0, SLICE_BLOCKS), jax.random.fold_in(key_of[4], 1), 0, SLICE_BLOCKS - 1).astype(jnp.int32)
    tile_live = touch_ends((jax.random.randint(key_of[5], (N_BLK, N_REP, PANEL_BLOCKS, TPR), 0, 5) < 2).astype(jnp.int32), jax.random.fold_in(key_of[5], 1), 0, 1)
    return dict(features=features, grad_out=grad_out, weight=weight, edge_tiles=edge_tiles, tile_cols=tile_cols, tile_live=tile_live)


def silu_slope(values):
    sigmoid_val = jax.nn.sigmoid(values)
    return sigmoid_val * (1.0 + values * (1.0 - sigmoid_val))

def pick_blocks(blocks, columns):
    return blocks[columns]

def reference(features, grad_out, weight, edge_tiles, tile_cols, tile_live):
    feat_width = features.shape[1]
    projected = jnp.dot(features, weight, preferred_element_type=jnp.float32).astype(jnp.bfloat16)
    by_slice = projected.reshape(N_BLK, N_REP, ROWS_DEV, feat_width).transpose(1, 0, 2, 3)
    by_slice = by_slice.reshape(N_REP, SLICE_BLOCKS, TILE, feat_width)
    masked = edge_tiles * tile_live[..., None, None].astype(edge_tiles.dtype)

    def panel_forward(inputs):
        panel_tiles, panel_cols = inputs
        picked = jax.vmap(pick_blocks)(by_slice, panel_cols)
        partial_value = jnp.einsum('rptij,rptjf->rpif', panel_tiles.astype(jnp.float32), picked.astype(jnp.float32))
        partial_value = lax.optimization_barrier(partial_value.astype(jnp.bfloat16)).astype(jnp.float32)
        return lax.optimization_barrier(jnp.sum(partial_value, axis=0))
    preact = lax.map(panel_forward, (masked, tile_cols)).reshape(NODES, feat_width)
    activations = jax.nn.silu(preact).astype(jnp.bfloat16)
    grad_preact = (grad_out.astype(jnp.float32) * silu_slope(preact)).astype(jnp.bfloat16)
    grad_panels = grad_preact.reshape(N_BLK, PANEL_BLOCKS, TILE, feat_width)

    def segment_blocks(products, columns):
        return jax.ops.segment_sum(products.reshape(-1, TILE, feat_width), columns.reshape(-1), num_segments=SLICE_BLOCKS)

    def panel_backward(running, inputs):
        panel_tiles, panel_cols, panel_grads = inputs
        products = jnp.einsum('rptij,pif->rptjf', panel_tiles.astype(jnp.float32), panel_grads.astype(jnp.float32))
        summed = jax.vmap(segment_blocks)(products, panel_cols)
        summed = lax.optimization_barrier(summed.astype(jnp.bfloat16)).astype(jnp.float32)
        return (running + summed, None)
    start_sum = jnp.zeros((N_REP, SLICE_BLOCKS, TILE, feat_width), jnp.float32)
    total, _ = lax.scan(panel_backward, start_sum, (masked, tile_cols, grad_panels))
    grad_projected = total.reshape(N_REP, N_BLK, ROWS_DEV, feat_width).transpose(1, 0, 2, 3)
    grad_projected = grad_projected.reshape(NODES, feat_width).astype(jnp.bfloat16)
    grad_features = jnp.dot(grad_projected, weight.T, preferred_element_type=jnp.float32).astype(jnp.bfloat16)
    grad_weight = jnp.dot(features.T, grad_projected, preferred_element_type=jnp.float32) * (1.0 / math.sqrt(NODES))
    return (activations, grad_features, grad_weight)
```

```python
import functools
import math

import jax
import jax.numpy as jnp
from jax import lax
from jax.experimental import pallas as pl
from jax.experimental.pallas import tpu as pltpu
from jax.sharding import PartitionSpec as P

MESH = pl.DeviceIdType.MESH
BF = jnp.bfloat16
F32 = jnp.float32
SIDE = 128
LANES = 128


def remote(src, dst, send, recv, where):
    return pltpu.make_async_remote_copy(
        src_ref=src, dst_ref=dst, send_sem=send, recv_sem=recv, device_id=where, device_id_type=MESH
    )


def kernel(
    nb, nr, scale,
    feat, gout, weight, tiles, cols, live, chain,
    act, gfeat, gwout,
    gath0, gath1, part, rsr, panel, runs, pair, snd, crl, crr, gp, featt, gloc, a1, a2, gw,
    ag_s, ag_r, rs_s, rs_r, pa_s, pa_r, pr_s, pr_r, ch_s, cl_r, cr_r, a1_s, a1_r, a2_s, a2_r, a3_s, a3_r,
):
    b = lax.axis_index("blk")
    r = lax.axis_index("rep")
    z = b // 2
    c = b % 2
    nz = nb // 2
    halves = feat.shape[1] // LANES
    bpd = feat.shape[0] // SIDE
    slots = tiles.shape[0]
    panel_blocks = nr * bpd
    per = slots // panel_blocks
    slice_blocks = nb * bpd
    gath = (gath0, gath1)
    sibling = b + 1 - 2 * c
    sp = part

    barrier = pltpu.get_barrier_semaphore()
    for k in range(1, nb):
        pl.semaphore_signal(barrier, inc=1, device_id={"blk": (b + k) % nb}, device_id_type=MESH)
    for k in range(1, nr):
        pl.semaphore_signal(barrier, inc=1, device_id={"rep": (r + k) % nr}, device_id_type=MESH)

    def project(h):
        def step(j, carry):
            rows = pl.ds(pl.multiple_of(j * SIDE, SIDE), SIDE)
            val = jnp.dot(feat[rows, :], weight[:, h * LANES:(h + 1) * LANES], preferred_element_type=F32)
            gath[h][b * bpd + j] = val.astype(BF)
            return carry
        lax.fori_loop(0, bpd, step, 0, unroll=2)
        gath[h][slice_blocks] = jnp.zeros((SIDE, LANES), BF)

    def ag_copy(h, way, slot, to):
        piece = gath[h].at[pl.ds(slot * bpd, bpd)]
        return remote(piece, piece, ag_s.at[h, way, slot], ag_r.at[h, slot], {"blk": to})

    def ag_own(h):
        @pl.when(z < nz - 1)
        def _():
            ag_copy(h, 0, b, b + 2).start()

        @pl.when(z > 0)
        def _():
            ag_copy(h, 1, b, b - 2).start()
        ag_copy(h, 2, b, sibling).start()

    def ag_relay(h, k):
        @pl.when(z - k >= 0)
        def _():
            slot = b - 2 * k
            ag_copy(h, 0, slot, sibling).wait_recv()

            @pl.when(z < nz - 1)
            def _():
                ag_copy(h, 0, slot, b + 2).start()
            ag_copy(h, 2, slot, sibling).start()

        @pl.when(z + k < nz)
        def _():
            slot = b + 2 * k
            ag_copy(h, 1, slot, sibling).wait_recv()

            @pl.when(z > 0)
            def _():
                ag_copy(h, 1, slot, b - 2).start()
            ag_copy(h, 2, slot, sibling).start()

    def ag_finish(h):
        for k in range(nz):
            ag_copy(h, 2, 2 * k + 1 - c, sibling).wait_recv()

    def ag_drain(h):
        for k in range(nz):
            slot = 2 * k + c

            @pl.when((k <= z) & (z < nz - 1))
            def _():
                ag_copy(h, 0, slot, sibling).wait_send()

            @pl.when((k >= z) & (z > 0))
            def _():
                ag_copy(h, 1, slot, sibling).wait_send()
            ag_copy(h, 2, slot, sibling).wait_send()

    def rs_copy(h, k):
        peer = (r + k) % nr
        return remote(
            part.at[h, pl.ds(peer * bpd, bpd)], rsr.at[h, r], rs_s.at[h, k], rs_r.at[h, r], {"rep": peer}
        )

    def rs_from(h, k):
        peer = (r + k) % nr
        return remote(
            part.at[h, pl.ds(peer * bpd, bpd)], rsr.at[h, peer], rs_s.at[h, k], rs_r.at[h, peer], {"rep": peer}
        )

    def forward(h):
        def shard(k, carry):
            peer = (r + k) % nr

            def block(j, inner):
                i = peer * bpd + j
                lhs, rhs = [], []
                for t in range(per):
                    s = i * per + t
                    on = live[s]
                    lhs.append(tiles[s])
                    rhs.append(gath[h][cols[s] * on + slice_blocks * (1 - on)])
                val = jnp.dot(
                    jnp.concatenate(lhs, axis=1), jnp.concatenate(rhs, axis=0), preferred_element_type=F32
                )
                part[h, i] = val.astype(BF)
                return inner
            lax.fori_loop(0, bpd, block, 0, unroll=True)

            @pl.when(k < nr)
            def _():
                rs_copy(h, k).start()
            return carry
        lax.fori_loop(1, nr + 1, shard, 0)

    def pa_copy(h, k):
        piece = panel.at[h, pl.ds(r * bpd, bpd)]
        return remote(piece, piece, pa_s.at[h, k], pa_r.at[h, r], {"rep": (r + k) % nr})

    def pa_from(h, k):
        peer = (r + k) % nr
        piece = panel.at[h, pl.ds(peer * bpd, bpd)]
        return remote(piece, piece, pa_s.at[h, k], pa_r.at[h, peer], {"rep": peer})

    def activate(h):
        for k in range(1, nr):
            rs_from(h, k).wait_recv()
        at = slice(h * LANES, (h + 1) * LANES)

        def step(j, carry):
            rows = pl.ds(pl.multiple_of(j * SIDE, SIDE), SIDE)
            val = part[h, r * bpd + j].astype(F32)
            for k in range(1, nr):
                val = val + rsr[h, (r + k) % nr, j].astype(F32)
            sig = jax.nn.sigmoid(val)
            act[rows, at] = (val * sig).astype(BF)
            slope = sig * (1.0 + val * (1.0 - sig))
            panel[h, r * bpd + j] = (gout[rows, at].astype(F32) * slope).astype(BF)
            return carry
        lax.fori_loop(0, bpd, step, 0)
        for k in range(1, nr):
            pa_copy(h, k).start()

    def pr_copy(h, d):
        return remote(
            sp.at[h, pl.ds((2 * d + 1 - c) * bpd, bpd)], pair.at[h, d], pr_s.at[h, d], pr_r.at[h, d],
            {"blk": sibling},
        )

    def backward(h):
        for k in range(1, nr):
            pa_from(h, k).wait_recv()
            rs_copy(h, k).wait_send()

        def step(i, carry):
            wide = jnp.concatenate([tiles[i * per + t] for t in range(per)], axis=1)
            prod = lax.dot_general(
                wide, panel[h, i], (((0,), (0,)), ((), ())), preferred_element_type=F32
            )
            for t in range(per):
                s = i * per + t
                runs[s] = prod[t * SIDE:(t + 1) * SIDE, :] + runs[chain[s]]
            return carry
        lax.fori_loop(0, panel_blocks, step, 0, unroll=2)

        def collect(shard):
            def move(j, carry):
                q = shard * bpd + j
                sp[h, q] = runs[chain[slots + q]].astype(BF)
                return carry
            lax.fori_loop(0, bpd, move, 0, unroll=2)

        for d in reversed(range(nz)):
            collect(2 * d + 1 - c)
            pr_copy(h, d).start()
        for d in range(nz):
            collect(2 * d + c)

    def right_copy(h, d):
        return remote(snd.at[h, d], crl.at[h, d], ch_s.at[h, d], cl_r.at[h, d], {"blk": b + 2})

    def left_copy(h, d):
        return remote(snd.at[h, d], crr.at[h, d], ch_s.at[h, d], cr_r.at[h, d], {"blk": b - 2})

    def merge(h, d, came):
        def step(j, carry):
            val = sp[h, (2 * d + c) * bpd + j].astype(F32) + pair[h, d, j].astype(F32)
            snd[h, d, j] = (val + came[h, d, j].astype(F32)).astype(BF)
            return carry
        lax.fori_loop(0, bpd, step, 0, unroll=2)

    def chain_step(h, t):
        right, left = nz - 1 - t, t

        @pl.when(z < right)
        def _():
            pr_copy(h, right).wait_recv()

            @pl.when(z > 0)
            def _():
                right_copy(h, right).wait_recv()
            merge(h, right, crl)
            right_copy(h, right).start()

        @pl.when(z > left)
        def _():
            pr_copy(h, left).wait_recv()

            @pl.when(z < nz - 1)
            def _():
                left_copy(h, left).wait_recv()
            merge(h, left, crr)
            left_copy(h, left).start()

    def a1_copy(h, k):
        peer = (b + k) % nb
        return remote(gloc.at[h, peer], a1.at[h, b], a1_s.at[h, k], a1_r.at[h, b], {"blk": peer})

    def a1_from(h, k):
        peer = (b + k) % nb
        return remote(gloc.at[h, peer], a1.at[h, peer], a1_s.at[h, k], a1_r.at[h, peer], {"blk": peer})

    def a2_copy(h, k):
        return remote(a2.at[h, r], a2.at[h, r], a2_s.at[h, k], a2_r.at[h, r], {"rep": (r + k) % nr})

    def a2_from(h, k):
        peer = (r + k) % nr
        return remote(a2.at[h, peer], a2.at[h, peer], a2_s.at[h, k], a2_r.at[h, peer], {"rep": peer})

    def a3_copy(h, k):
        return remote(gw.at[h, b], gw.at[h, b], a3_s.at[h, k], a3_r.at[h, b], {"blk": (b + k) % nb})

    def a3_from(h, k):
        peer = (b + k) % nb
        return remote(gw.at[h, peer], gw.at[h, peer], a3_s.at[h, k], a3_r.at[h, peer], {"blk": peer})

    def chain_finish(h):
        pr_copy(h, z).wait_recv()

        @pl.when(z > 0)
        def _():
            right_copy(h, z).wait_recv()

        @pl.when(z < nz - 1)
        def _():
            left_copy(h, z).wait_recv()

        at = slice(h * LANES, (h + 1) * LANES)

        def step(j, carry):
            rows = pl.ds(pl.multiple_of(j * SIDE, SIDE), SIDE)
            val = sp[h, b * bpd + j].astype(F32) + pair[h, z, j].astype(F32)
            val = val + crl[h, z, j].astype(F32) + crr[h, z, j].astype(F32)
            gp[rows, at] = val.astype(BF)
            return carry
        lax.fori_loop(0, bpd, step, 0, unroll=2)
        share = feat.shape[1] // nb
        for p in range(nb):
            val = jnp.dot(featt[p * share:(p + 1) * share, :], gp[:, at], preferred_element_type=F32)
            gloc[h, p] = val.astype(BF)
        for k in range(1, nb):
            a1_copy(h, k).start()

    def reduce_two(h):
        for k in range(1, nb):
            a1_from(h, k).wait_recv()
        val = gloc[h, b].astype(F32)
        for k in range(1, nb):
            val = val + a1[h, (b + k) % nb].astype(F32)
        a2[h, r] = val.astype(BF)
        for k in range(1, nr):
            a2_copy(h, k).start()

    def reduce_three(h):
        for k in range(1, nr):
            a2_from(h, k).wait_recv()
        val = a2[h, 0].astype(F32)
        for k in range(1, nr):
            val = val + a2[h, k].astype(F32)
        gw[h, b] = val.astype(BF)
        for k in range(1, nb):
            a3_copy(h, k).start()

    def reduce_end(h):
        for k in range(1, nb):
            a3_from(h, k).wait_recv()
        share = feat.shape[1] // nb
        for p in range(nb):
            gwout[p * share:(p + 1) * share, h * LANES:(h + 1) * LANES] = gw[h, p].astype(F32) * scale

    def drain(h):
        ag_drain(h)
        for k in range(1, nr):
            pa_copy(h, k).wait_send()
            a2_copy(h, k).wait_send()
        for k in range(1, nb):
            a1_copy(h, k).wait_send()
            a3_copy(h, k).wait_send()
        for d in range(nz):
            pr_copy(h, d).wait_send()

            @pl.when(z != d)
            def _():
                right_copy(h, d).wait_send()

    project(0)
    pl.semaphore_wait(barrier, nb - 1 + nr - 1)
    ag_own(0)
    project(1)
    runs[slots] = jnp.zeros((SIDE, LANES), F32)
    featt[...] = feat[...].T

    @pl.when(z == 0)
    def _():
        crl[...] = jnp.zeros(crl.shape, BF)

    @pl.when(z == nz - 1)
    def _():
        crr[...] = jnp.zeros(crr.shape, BF)

    for k in range(1, nz):
        ag_relay(0, k)
    ag_own(1)
    ag_finish(0)
    forward(0)
    for k in range(1, nz - 1):
        ag_relay(1, k)
    activate(0)
    ag_relay(1, nz - 1)
    ag_finish(1)
    forward(1)
    backward(0)
    chain_step(0, 0)
    activate(1)
    for t in range(1, nz - 1):
        chain_step(0, t)
    backward(1)
    chain_finish(0)
    chain_step(1, 0)
    reduce_two(0)
    for t in range(1, nz - 1):
        chain_step(1, t)
    reduce_three(0)
    chain_finish(1)

    def out_rows(j, carry):
        rows = pl.ds(pl.multiple_of(j * SIDE, SIDE), SIDE)
        val = lax.dot_general(gp[rows, :], weight[...], (((1,), (1,)), ((), ())), preferred_element_type=F32)
        gfeat[rows, :] = val.astype(BF)
        return carry
    lax.fori_loop(0, bpd, out_rows, 0, unroll=2)
    reduce_two(1)
    reduce_end(0)
    reduce_three(1)
    drain(0)
    reduce_end(1)
    drain(1)


def per_device(nb, nr, features, grad_out, weight, edge_tiles, tile_cols, tile_live):
    rows, width = features.shape
    side = edge_tiles.shape[-1]
    bpd = rows // side
    tiles = edge_tiles.reshape(-1, side, side)
    slots = tiles.shape[0]
    cols = tile_cols.reshape(-1)
    live = tile_live.reshape(-1)
    blocks = nb * bpd
    halves = width // LANES
    nz = nb // 2
    share = width // nb
    order = jnp.arange(slots, dtype=jnp.int32)
    keys = jnp.concatenate([cols, jnp.arange(blocks, dtype=jnp.int32)])
    limit = jnp.concatenate([order, jnp.full((blocks,), slots, jnp.int32)])
    hit = (keys[:, None] == cols[None, :]) & (live[None, :] == 1) & (order[None, :] < limit[:, None])
    chain = jnp.max(jnp.where(hit, order[None, :], -1), axis=1)
    chain = jnp.where(chain < 0, slots, chain)

    vm = pl.BlockSpec(memory_space=pltpu.VMEM)
    sm = pl.BlockSpec(memory_space=pltpu.SMEM)
    block = (SIDE, LANES)
    dma = pltpu.SemaphoreType.DMA
    scratch = [
        pltpu.VMEM((blocks + 1,) + block, BF),
        pltpu.VMEM((blocks + 1,) + block, BF),
        pltpu.VMEM((halves, max(blocks, nr * bpd)) + block, BF),
        pltpu.VMEM((halves, nr, bpd) + block, BF),
        pltpu.VMEM((halves, nr * bpd) + block, BF),
        pltpu.VMEM((slots + 1,) + block, F32),
        pltpu.VMEM((halves, nz, bpd) + block, BF),
        pltpu.VMEM((halves, nz, bpd) + block, BF),
        pltpu.VMEM((halves, nz, bpd) + block, BF),
        pltpu.VMEM((halves, nz, bpd) + block, BF),
        pltpu.VMEM((rows, width), BF),
        pltpu.VMEM((width, rows), BF),
        pltpu.VMEM((halves, nb, share, LANES), BF),
        pltpu.VMEM((halves, nb, share, LANES), BF),
        pltpu.VMEM((halves, nr, share, LANES), BF),
        pltpu.VMEM((halves, nb, share, LANES), BF),
        dma((halves, 3, nb)), dma((halves, nb)),
        dma((halves, nr)), dma((halves, nr)),
        dma((halves, nr)), dma((halves, nr)),
        dma((halves, nz)), dma((halves, nz)),
        dma((halves, nz)), dma((halves, nz)), dma((halves, nz)),
        dma((halves, nb)), dma((halves, nb)),
        dma((halves, nr)), dma((halves, nr)),
        dma((halves, nb)), dma((halves, nb)),
    ]
    scale = 1.0 / math.sqrt(rows * nb * nr)
    return pl.pallas_call(
        functools.partial(kernel, nb, nr, scale),
        out_shape=(
            jax.ShapeDtypeStruct((rows, width), BF),
            jax.ShapeDtypeStruct((rows, width), BF),
            jax.ShapeDtypeStruct((width, width), F32),
        ),
        in_specs=[vm, vm, vm, vm, sm, sm, sm],
        out_specs=(vm, vm, vm),
        scratch_shapes=scratch,
        compiler_params=pltpu.CompilerParams(
            collective_id=0, has_side_effects=True, vmem_limit_bytes=61 * 1024 * 1024
        ),
    )(features, grad_out, weight, tiles, cols, live, chain)


def solution(mesh):
    placed = (
        P(("blk", "rep"), None),
        P(("blk", "rep"), None),
        P(),
        P("blk", "rep", None, None, None, None),
        P("blk", "rep", None, None),
        P("blk", "rep", None, None),
    )
    return jax.shard_map(
        functools.partial(per_device, mesh.shape["blk"], mesh.shape["rep"]),
        mesh=mesh,
        in_specs=placed,
        out_specs=(P(("blk", "rep"), None), P(("blk", "rep"), None), P()),
        check_vma=False,
    )
```

```python
import functools
import math

import jax
import jax.numpy as jnp
from jax import lax
from jax.experimental import pallas as pl
from jax.experimental.pallas import tpu as pltpu
from jax.sharding import PartitionSpec as P

MESH = pl.DeviceIdType.MESH
BF = jnp.bfloat16
F32 = jnp.float32
SIDE = 128
LANES = 128


def remote(src, dst, send, recv, where):
    return pltpu.make_async_remote_copy(
        src_ref=src, dst_ref=dst, send_sem=send, recv_sem=recv, device_id=where, device_id_type=MESH
    )


def kernel(
    nb, nr, scale,
    feat, gout, weight, tiles, cols, live, chain,
    act, gfeat, gwout,
    gath0, gath1, part, rsr, panel, runs, pair, snd, crl, crr, gp, featt, turned, gloc, a1, a2, gw,
    ag_s, ag_r, rs_s, rs_r, pa_s, pa_r, pr_s, pr_r, ch_s, cl_r, cr_r, a1_s, a1_r, a2_s, a2_r, a3_s, a3_r,
):
    b = lax.axis_index("blk")
    r = lax.axis_index("rep")
    z = b // 2
    c = b % 2
    nz = nb // 2
    halves = feat.shape[1] // LANES
    bpd = feat.shape[0] // SIDE
    slots = tiles.shape[0]
    panel_blocks = nr * bpd
    per = slots // panel_blocks
    slice_blocks = nb * bpd
    gath = (gath0, gath1)
    sibling = b + 1 - 2 * c
    sp = part

    barrier = pltpu.get_barrier_semaphore()
    for k in range(1, nb):
        pl.semaphore_signal(barrier, inc=1, device_id={"blk": (b + k) % nb}, device_id_type=MESH)
    for k in range(1, nr):
        pl.semaphore_signal(barrier, inc=1, device_id={"rep": (r + k) % nr}, device_id_type=MESH)

    def project(h):
        def step(j, carry):
            rows = pl.ds(pl.multiple_of(j * SIDE, SIDE), SIDE)
            val = jnp.dot(feat[rows, :], weight[:, h * LANES:(h + 1) * LANES], preferred_element_type=F32)
            gath[h][b * bpd + j] = val.astype(BF)
            return carry
        lax.fori_loop(0, bpd, step, 0, unroll=2)
        gath[h][slice_blocks] = jnp.zeros((SIDE, LANES), BF)

    def ag_copy(h, way, slot, to):
        piece = gath[h].at[pl.ds(slot * bpd, bpd)]
        return remote(piece, piece, ag_s.at[h, way, slot], ag_r.at[h, slot], {"blk": to})

    def ag_own(h):
        @pl.when(z < nz - 1)
        def _():
            ag_copy(h, 0, b, b + 2).start()

        @pl.when(z > 0)
        def _():
            ag_copy(h, 1, b, b - 2).start()
        ag_copy(h, 2, b, sibling).start()

    def ag_relay(h, k):
        @pl.when(z - k >= 0)
        def _():
            slot = b - 2 * k
            ag_copy(h, 0, slot, sibling).wait_recv()

            @pl.when(z < nz - 1)
            def _():
                ag_copy(h, 0, slot, b + 2).start()
            ag_copy(h, 2, slot, sibling).start()

        @pl.when(z + k < nz)
        def _():
            slot = b + 2 * k
            ag_copy(h, 1, slot, sibling).wait_recv()

            @pl.when(z > 0)
            def _():
                ag_copy(h, 1, slot, b - 2).start()
            ag_copy(h, 2, slot, sibling).start()

    def ag_finish(h):
        for k in range(nz):
            ag_copy(h, 2, 2 * k + 1 - c, sibling).wait_recv()

    def ag_drain(h):
        for k in range(nz):
            slot = 2 * k + c

            @pl.when((k <= z) & (z < nz - 1))
            def _():
                ag_copy(h, 0, slot, sibling).wait_send()

            @pl.when((k >= z) & (z > 0))
            def _():
                ag_copy(h, 1, slot, sibling).wait_send()
            ag_copy(h, 2, slot, sibling).wait_send()

    def rs_copy(h, k):
        peer = (r + k) % nr
        return remote(
            part.at[h, pl.ds(peer * bpd, bpd)], rsr.at[h, r], rs_s.at[h, k], rs_r.at[h, r], {"rep": peer}
        )

    def rs_from(h, k):
        peer = (r + k) % nr
        return remote(
            part.at[h, pl.ds(peer * bpd, bpd)], rsr.at[h, peer], rs_s.at[h, k], rs_r.at[h, peer], {"rep": peer}
        )

    def forward(h):
        def shard(k, carry):
            peer = (r + k) % nr

            def block(j, inner):
                i = peer * bpd + j
                lhs, rhs = [], []
                for t in range(per):
                    s = i * per + t
                    on = live[s]
                    lhs.append(tiles[s])
                    rhs.append(gath[h][cols[s] * on + slice_blocks * (1 - on)])
                val = jnp.dot(
                    jnp.concatenate(lhs, axis=1), jnp.concatenate(rhs, axis=0), preferred_element_type=F32
                )
                part[h, i] = val.astype(BF)
                return inner
            lax.fori_loop(0, bpd, block, 0, unroll=True)

            @pl.when(k < nr)
            def _():
                rs_copy(h, k).start()
            return carry
        lax.fori_loop(1, nr + 1, shard, 0)

    def pa_copy(h, k):
        piece = panel.at[h, pl.ds(r * bpd, bpd)]
        return remote(piece, piece, pa_s.at[h, k], pa_r.at[h, r], {"rep": (r + k) % nr})

    def pa_from(h, k):
        peer = (r + k) % nr
        piece = panel.at[h, pl.ds(peer * bpd, bpd)]
        return remote(piece, piece, pa_s.at[h, k], pa_r.at[h, peer], {"rep": peer})

    def activate(h):
        for k in range(1, nr):
            rs_from(h, k).wait_recv()
        at = slice(h * LANES, (h + 1) * LANES)

        def step(j, carry):
            rows = pl.ds(pl.multiple_of(j * SIDE, SIDE), SIDE)
            val = part[h, r * bpd + j].astype(F32)
            for k in range(1, nr):
                val = val + rsr[h, (r + k) % nr, j].astype(F32)
            sig = jax.nn.sigmoid(val)
            act[rows, at] = (val * sig).astype(BF)
            slope = sig * (1.0 + val * (1.0 - sig))
            panel[h, r * bpd + j] = (gout[rows, at].astype(F32) * slope).astype(BF)
            return carry
        lax.fori_loop(0, bpd, step, 0)
        for k in range(1, nr):
            pa_copy(h, k).start()

    def pr_copy(h, d):
        return remote(
            sp.at[h, pl.ds((2 * d + 1 - c) * bpd, bpd)], pair.at[h, d], pr_s.at[h, d], pr_r.at[h, d],
            {"blk": sibling},
        )

    def backward(h):
        for k in range(1, nr):
            pa_from(h, k).wait_recv()
            rs_copy(h, k).wait_send()

        def step(i, carry):
            if turned.shape[0] == panel_blocks:
                prod = jnp.dot(turned[i], panel[h, i], preferred_element_type=F32)
            else:
                wide = jnp.concatenate([tiles[i * per + t] for t in range(per)], axis=1)
                prod = lax.dot_general(
                    wide, panel[h, i], (((0,), (0,)), ((), ())), preferred_element_type=F32
                )
            for t in range(per):
                runs[i * per + t] = prod[t * SIDE:(t + 1) * SIDE, :]
            return carry
        lax.fori_loop(0, panel_blocks, step, 0, unroll=4)

        def link(s, carry):
            runs[s] = runs[s] + runs[chain[s]]
            return carry
        lax.fori_loop(0, slots, link, 0, unroll=2)

        def collect(shard):
            def move(j, carry):
                q = shard * bpd + j
                sp[h, q] = runs[chain[slots + q]].astype(BF)
                return carry
            lax.fori_loop(0, bpd, move, 0, unroll=2)

        for d in reversed(range(nz)):
            collect(2 * d + 1 - c)
            pr_copy(h, d).start()
        for d in range(nz):
            collect(2 * d + c)

    def right_copy(h, d):
        return remote(snd.at[h, d], crl.at[h, d], ch_s.at[h, d], cl_r.at[h, d], {"blk": b + 2})

    def left_copy(h, d):
        return remote(snd.at[h, d], crr.at[h, d], ch_s.at[h, d], cr_r.at[h, d], {"blk": b - 2})

    def merge(h, d, came):
        def step(j, carry):
            val = sp[h, (2 * d + c) * bpd + j].astype(F32) + pair[h, d, j].astype(F32)
            snd[h, d, j] = (val + came[h, d, j].astype(F32)).astype(BF)
            return carry
        lax.fori_loop(0, bpd, step, 0, unroll=2)

    def chain_step(h, t):
        right, left = nz - 1 - t, t

        @pl.when(z < right)
        def _():
            pr_copy(h, right).wait_recv()

            @pl.when(z > 0)
            def _():
                right_copy(h, right).wait_recv()
            merge(h, right, crl)
            right_copy(h, right).start()

        @pl.when(z > left)
        def _():
            pr_copy(h, left).wait_recv()

            @pl.when(z < nz - 1)
            def _():
                left_copy(h, left).wait_recv()
            merge(h, left, crr)
            left_copy(h, left).start()

    def a1_copy(h, k):
        peer = (b + k) % nb
        return remote(gloc.at[h, peer], a1.at[h, b], a1_s.at[h, k], a1_r.at[h, b], {"blk": peer})

    def a1_from(h, k):
        peer = (b + k) % nb
        return remote(gloc.at[h, peer], a1.at[h, peer], a1_s.at[h, k], a1_r.at[h, peer], {"blk": peer})

    def a2_copy(h, k):
        return remote(a2.at[h, r], a2.at[h, r], a2_s.at[h, k], a2_r.at[h, r], {"rep": (r + k) % nr})

    def a2_from(h, k):
        peer = (r + k) % nr
        return remote(a2.at[h, peer], a2.at[h, peer], a2_s.at[h, k], a2_r.at[h, peer], {"rep": peer})

    def a3_copy(h, k):
        return remote(gw.at[h, b], gw.at[h, b], a3_s.at[h, k], a3_r.at[h, b], {"blk": (b + k) % nb})

    def a3_from(h, k):
        peer = (b + k) % nb
        return remote(gw.at[h, peer], gw.at[h, peer], a3_s.at[h, k], a3_r.at[h, peer], {"blk": peer})

    def chain_finish(h):
        pr_copy(h, z).wait_recv()

        @pl.when(z > 0)
        def _():
            right_copy(h, z).wait_recv()

        @pl.when(z < nz - 1)
        def _():
            left_copy(h, z).wait_recv()

        at = slice(h * LANES, (h + 1) * LANES)

        def step(j, carry):
            rows = pl.ds(pl.multiple_of(j * SIDE, SIDE), SIDE)
            val = sp[h, b * bpd + j].astype(F32) + pair[h, z, j].astype(F32)
            val = val + crl[h, z, j].astype(F32) + crr[h, z, j].astype(F32)
            gp[rows, at] = val.astype(BF)
            return carry
        lax.fori_loop(0, bpd, step, 0, unroll=2)
        share = feat.shape[1] // nb
        for p in range(nb):
            val = jnp.dot(featt[p * share:(p + 1) * share, :], gp[:, at], preferred_element_type=F32)
            gloc[h, p] = val.astype(BF)
        for k in range(1, nb):
            a1_copy(h, k).start()

    def reduce_two(h):
        for k in range(1, nb):
            a1_from(h, k).wait_recv()
        val = gloc[h, b].astype(F32)
        for k in range(1, nb):
            val = val + a1[h, (b + k) % nb].astype(F32)
        a2[h, r] = val.astype(BF)
        for k in range(1, nr):
            a2_copy(h, k).start()

    def reduce_three(h):
        for k in range(1, nr):
            a2_from(h, k).wait_recv()
        val = a2[h, 0].astype(F32)
        for k in range(1, nr):
            val = val + a2[h, k].astype(F32)
        gw[h, b] = val.astype(BF)
        for k in range(1, nb):
            a3_copy(h, k).start()

    def reduce_end(h):
        for k in range(1, nb):
            a3_from(h, k).wait_recv()
        share = feat.shape[1] // nb
        for p in range(nb):
            gwout[p * share:(p + 1) * share, h * LANES:(h + 1) * LANES] = gw[h, p].astype(F32) * scale

    def drain(h):
        ag_drain(h)
        for k in range(1, nr):
            pa_copy(h, k).wait_send()
            a2_copy(h, k).wait_send()
        for k in range(1, nb):
            a1_copy(h, k).wait_send()
            a3_copy(h, k).wait_send()
        for d in range(nz):
            pr_copy(h, d).wait_send()

            @pl.when(z != d)
            def _():
                right_copy(h, d).wait_send()

    project(0)
    pl.semaphore_wait(barrier, nb - 1 + nr - 1)
    ag_own(0)
    project(1)
    runs[slots] = jnp.zeros((SIDE, LANES), F32)
    featt[...] = feat[...].T

    @pl.when(z == 0)
    def _():
        crl[...] = jnp.zeros(crl.shape, BF)

    @pl.when(z == nz - 1)
    def _():
        crr[...] = jnp.zeros(crr.shape, BF)

    ag_relay(0, 1)
    if turned.shape[0] == panel_blocks:
        def turn(i, carry):
            for t in range(per):
                turned[i, t * SIDE:(t + 1) * SIDE, :] = tiles[i * per + t].T
            return carry
        lax.fori_loop(0, panel_blocks, turn, 0, unroll=2)
    for k in range(2, nz):
        ag_relay(0, k)
    ag_own(1)
    ag_finish(0)
    forward(0)
    for k in range(1, nz - 1):
        ag_relay(1, k)
    activate(0)
    ag_relay(1, nz - 1)
    ag_finish(1)
    forward(1)
    backward(0)
    chain_step(0, 0)
    activate(1)
    for t in range(1, nz - 1):
        chain_step(0, t)
    backward(1)
    chain_finish(0)
    chain_step(1, 0)
    reduce_two(0)
    for t in range(1, nz - 1):
        chain_step(1, t)
    reduce_three(0)
    chain_finish(1)

    def out_rows(j, carry):
        rows = pl.ds(pl.multiple_of(j * SIDE, SIDE), SIDE)
        val = lax.dot_general(gp[rows, :], weight[...], (((1,), (1,)), ((), ())), preferred_element_type=F32)
        gfeat[rows, :] = val.astype(BF)
        return carry
    lax.fori_loop(0, bpd, out_rows, 0, unroll=2)
    reduce_two(1)
    reduce_end(0)
    reduce_three(1)
    drain(0)
    reduce_end(1)
    drain(1)


def per_device(nb, nr, features, grad_out, weight, edge_tiles, tile_cols, tile_live):
    rows, width = features.shape
    side = edge_tiles.shape[-1]
    bpd = rows // side
    tiles = edge_tiles.reshape(-1, side, side)
    slots = tiles.shape[0]
    cols = tile_cols.reshape(-1)
    live = tile_live.reshape(-1)
    blocks = nb * bpd
    halves = width // LANES
    nz = nb // 2
    share = width // nb
    order = jnp.arange(slots, dtype=jnp.int32)
    keys = jnp.concatenate([cols, jnp.arange(blocks, dtype=jnp.int32)])
    limit = jnp.concatenate([order, jnp.full((blocks,), slots, jnp.int32)])
    hit = (keys[:, None] == cols[None, :]) & (live[None, :] == 1) & (order[None, :] < limit[:, None])
    chain = jnp.max(jnp.where(hit, order[None, :], -1), axis=1)
    chain = jnp.where(chain < 0, slots, chain)

    vm = pl.BlockSpec(memory_space=pltpu.VMEM)
    sm = pl.BlockSpec(memory_space=pltpu.SMEM)
    block = (SIDE, LANES)
    dma = pltpu.SemaphoreType.DMA
    scratch = [
        pltpu.VMEM((blocks + 1,) + block, BF),
        pltpu.VMEM((blocks + 1,) + block, BF),
        pltpu.VMEM((halves, max(blocks, nr * bpd)) + block, BF),
        pltpu.VMEM((halves, nr, bpd) + block, BF),
        pltpu.VMEM((halves, nr * bpd) + block, BF),
        pltpu.VMEM((slots + 1,) + block, F32),
        pltpu.VMEM((halves, nz, bpd) + block, BF),
        pltpu.VMEM((halves, nz, bpd) + block, BF),
        pltpu.VMEM((halves, nz, bpd) + block, BF),
        pltpu.VMEM((halves, nz, bpd) + block, BF),
        pltpu.VMEM((rows, width), BF),
        pltpu.VMEM((width, rows), BF),
        pltpu.VMEM((nr * bpd if slots <= 64 else 1, slots // (nr * bpd) * SIDE, SIDE), BF),
        pltpu.VMEM((halves, nb, share, LANES), BF),
        pltpu.VMEM((halves, nb, share, LANES), BF),
        pltpu.VMEM((halves, nr, share, LANES), BF),
        pltpu.VMEM((halves, nb, share, LANES), BF),
        dma((halves, 3, nb)), dma((halves, nb)),
        dma((halves, nr)), dma((halves, nr)),
        dma((halves, nr)), dma((halves, nr)),
        dma((halves, nz)), dma((halves, nz)),
        dma((halves, nz)), dma((halves, nz)), dma((halves, nz)),
        dma((halves, nb)), dma((halves, nb)),
        dma((halves, nr)), dma((halves, nr)),
        dma((halves, nb)), dma((halves, nb)),
    ]
    scale = 1.0 / math.sqrt(rows * nb * nr)
    return pl.pallas_call(
        functools.partial(kernel, nb, nr, scale),
        out_shape=(
            jax.ShapeDtypeStruct((rows, width), BF),
            jax.ShapeDtypeStruct((rows, width), BF),
            jax.ShapeDtypeStruct((width, width), F32),
        ),
        in_specs=[vm, vm, vm, vm, sm, sm, sm],
        out_specs=(vm, vm, vm),
        scratch_shapes=scratch,
        compiler_params=pltpu.CompilerParams(
            collective_id=0, has_side_effects=True, vmem_limit_bytes=61 * 1024 * 1024
        ),
    )(features, grad_out, weight, tiles, cols, live, chain)


def solution(mesh):
    placed = (
        P(("blk", "rep"), None),
        P(("blk", "rep"), None),
        P(),
        P("blk", "rep", None, None, None, None),
        P("blk", "rep", None, None),
        P("blk", "rep", None, None),
    )
    return jax.shard_map(
        functools.partial(per_device, mesh.shape["blk"], mesh.shape["rep"]),
        mesh=mesh,
        in_specs=placed,
        out_specs=(P(("blk", "rep"), None), P(("blk", "rep"), None), P()),
        check_vma=False,
    )
```
